32 devices in a mesh: grp: 2 (over y), row: 4 (over z), head: 4 (over x, core).
Axes of the slice: x: 2, y: 2, z: 4, core: 2. Of those that a mesh axis runs over, the one named last changes fastest.
Arguments:
- prefill_kv: bfloat16 [1024, 8, 2, 8, 128], P(('grp', 'row'), None, None, 'head'), parts along dimension 0, may hold values from -6 to 6
- page_table: int32 [1024], P(('grp', 'row')), parts along dimension 0, may hold values from 0 to 511, as said below
- prompt_lengths: int32 [16], P('grp'), parts along dimension 0, may hold values from 1 to 128, 512 in all
- prompt_query: bfloat16 [16, 64, 128], P('grp', 'head'), parts along dimension 0, may hold values from -200 to 200
- prompt_new: bfloat16 [16, 2, 8, 128], P('grp', None, 'head'), parts along dimension 0, may hold values from -6 to 6
- decode_query: bfloat16 [16, 64, 128], P(('grp', 'row'), 'head'), parts along dimension 0, may hold values from -200 to 200
- decode_new: bfloat16 [16, 2, 8, 128], P(('grp', 'row'), None, 'head'), parts along dimension 0, may hold values from -6 to 6
- decode_cache: bfloat16 [16, 256, 2, 8, 128], P(('grp', 'row'), None, None, 'head'), parts along dimension 0, may hold values from -6 to 6
- cached_lengths: int32 [16], P(('grp', 'row')), parts along dimension 0, may hold values from 1 to 256, as said below
Outputs:
- decode_out: bfloat16 [16, 8192], P(('grp', 'row'), 'head'), parts along dimension 0
- prompt_out: bfloat16 [16, 8192], P('grp', 'head'), parts along dimension 0
- kv_pool: bfloat16 [1024, 8, 2, 8, 128], P(('grp', 'row'), None, None, 'head'), parts along dimension 0
The draws below stay inside these ranges and needn't reach their ends.
There are 2 independent parts, one for each index of `grp`. The reference program is written for one: setup_inputs(seed, part) draws one part's arguments, and reference() takes and returns one part's arrays. A program takes and returns all parts, laid end to end along the dimension named above; each array names one. Nothing has to cross between parts.
Inputs may be any that keep to these rules, and one draw needn't show every extreme that they name: `page_table`: entries are distinct and cover every pool slot. For a page on device s of row (p // 128 = s), the entry e satisfies (e % 128) // 32 = s: a page goes to device e // 128, into one of the 32 slots that this device keeps for s, so every device sends exactly 32 pages to every device. `prompt_lengths`: the lengths sum to 512; one prompt has exactly 128 pages. `cached_lengths`: some decode sequence uses all 256 positions.
All inputs are finite; a program needn't handle non-finite values.
Results may differ from the reference program's by a relative error of at most 0.0035.
Values may be sent and summed in bfloat16 or wider, within the bound.
A program may use at most 64 MiB of HBM per device.

```python
import math
import jax
import jax.numpy as jnp
import numpy as np
from jax import lax

QH = 64
KVH = 8
HD = 128
PAGE = 8
PROMPTS = 8
PP_DEV = 128
PAGES = 512
POOL_DEV = 128
MOST_PAGES = 128
SEQS = 8
CACHE = 256
N_ROW = 4


def own_keys(key, salt, row_count):
    noise = jax.random.normal(jax.random.fold_in(key, salt), (row_count, KVH, HD), jnp.float32)
    return jnp.clip(noise, -6.0, 6.0)


def drawn_queries(key, row_count):
    noise = jax.random.normal(key, (row_count, QH, HD), jnp.float32)
    return jnp.clip(noise, -5.0, 5.0) * 5.0


def draw_prompt_query(key, part):
    key = jax.random.fold_in(key, 22)
    queries = drawn_queries(key, PROMPTS)
    return queries.astype(jnp.bfloat16)


def draw_prompt_new(key, part):
    keys_own = own_keys(key, 101, PROMPTS)
    key = jax.random.fold_in(key, 21)
    value_rows = jnp.clip(jax.random.normal(key, (PROMPTS, KVH, HD), jnp.float32), -6.0, 6.0)
    return jnp.stack([keys_own, value_rows], axis=1).astype(jnp.bfloat16)


def draw_decode_query(key, part):
    key = jax.random.fold_in(key, 24)
    queries = drawn_queries(key, SEQS)
    return queries.astype(jnp.bfloat16)


def draw_decode_new(key, part):
    keys_own = own_keys(key, 202, SEQS)
    key = jax.random.fold_in(key, 23)
    value_rows = jnp.clip(jax.random.normal(key, (SEQS, KVH, HD), jnp.float32), -6.0, 6.0)
    return jnp.stack([keys_own, value_rows], axis=1).astype(jnp.bfloat16)


def draw_cached_lengths(key, part):
    key = jax.random.fold_in(key, 31)
    first_key, spot_key = jax.random.split(key)
    drawn = jax.random.randint(first_key, (SEQS,), 1, CACHE + 1, jnp.int32)
    spot_index = jax.random.randint(spot_key, (), 0, SEQS, jnp.int32)
    return drawn.at[spot_index].set(CACHE).astype(jnp.int32)


def draw_page_table(key, part):
    key = jax.random.fold_in(key, 11)
    pool_slots = PP_DEV
    per_pair = pool_slots // N_ROW
    chosen = jax.vmap(lambda small: jax.random.permutation(small, pool_slots))(jax.random.split(key, N_ROW)).astype(jnp.int32)
    dest_ids = chosen // per_pair
    lane_ids = chosen % per_pair
    source_ids = jnp.arange(N_ROW, dtype=jnp.int32)[:, None]
    table = dest_ids * pool_slots + source_ids * per_pair + lane_ids
    return table.reshape(-1).astype(jnp.int32)


def levels(stream_key, shape, cuts, smallest, high):
    gain, own = 1.0, jax.random.fold_in(stream_key, 6)
    for dim, shards_of in cuts:
        heights = jnp.exp(jax.random.uniform(jax.random.fold_in(own, dim), (shards_of,), jnp.float32, smallest / len(cuts), high / len(cuts)))
        gain = gain * jnp.repeat(heights, shape[dim] // shards_of).reshape([-1 if axis == dim else 1 for axis in range(len(shape))])
    return gain


def split_up(amount, total, bound, lean):
    weights = [(1 << 20) // math.isqrt(rank ** lean) + 1 for rank in range(2, amount + 1)]
    spare, given = total - bound - (amount - 1), [1] * (amount - 1)
    while spare > 0:
        free = [i for i in range(amount - 1) if given[i] < bound]
        pool, remaining = sum([weights[i] for i in free]), spare
        for i in free:
            extra = min(bound - given[i], max(1, remaining * weights[i] // pool), spare)
            given[i] = given[i] + extra
            spare = spare - extra
    return np.array([bound] + given)


def ragged_sizes(key, count, total, bound, lean):
    if count == 2:
        one = jax.random.randint(key, (), max(1, total - bound), min(bound, total - 1) + 1)
        return jnp.stack([one, total - one])
    lengths = jnp.asarray(split_up(count, total, bound, lean), jnp.int32)
    couples = (count - 1) // 2
    giver, receiver = lengths[1:1 + 2 * couples:2], lengths[2:2 + 2 * couples:2]
    margin = jnp.minimum(giver - 1, bound - receiver)
    shifted = jax.random.randint(jax.random.fold_in(key, 1), (couples,), 0, 1 << 20) % (margin + 1)
    lengths = lengths.at[1:1 + 2 * couples:2].set(giver - shifted).at[2:2 + 2 * couples:2].set(receiver + shifted)
    return lengths[jax.random.permutation(jax.random.fold_in(key, 2), count)]


def normal_values(key, dims, deviation, most, cuts=(), kind=jnp.bfloat16):
    entries = jax.random.normal(key, dims, jnp.float32) * deviation
    if len(cuts) > 0:
        entries = levels(key, dims, cuts, -0.22, 0.18) * entries
    return jnp.clip(entries, min=-most, max=most).astype(kind)


def setup_inputs(seed: int = 0, part: int = 0) -> dict:
    key_of = jax.random.split(jax.random.key(seed), 10)
    part_keys = jax.random.split(jax.random.fold_in(key_of[9], part), 10)
    prefill_kv = normal_values(part_keys[0], (PAGES, PAGE, 2, KVH, HD), 1.0, 6.0, ((0, 4), (3, 4)))
    page_table = draw_page_table(jax.random.fold_in(jax.random.fold_in(key_of[9], part), 71), part)
    prompt_lengths = ragged_sizes(part_keys[2], PROMPTS, PAGES, MOST_PAGES, 2).astype(jnp.int32)
    prompt_query = draw_prompt_query(jax.random.fold_in(jax.random.fold_in(key_of[9], part), 71), part)
    prompt_new = draw_prompt_new(jax.random.fold_in(jax.random.fold_in(key_of[9], part), 71), part)
    decode_query = draw_decode_query(jax.random.fold_in(jax.random.fold_in(key_of[9], part), 71), part)
    decode_new = draw_decode_new(jax.random.fold_in(jax.random.fold_in(key_of[9], part), 71), part)
    decode_cache = normal_values(part_keys[7], (SEQS, CACHE, 2, KVH, HD), 1.0, 6.0, ((0, 4), (3, 4)))
    cached_lengths = draw_cached_lengths(jax.random.fold_in(jax.random.fold_in(key_of[9], part), 71), part)
    return dict(prefill_kv=prefill_kv, page_table=page_table, prompt_lengths=prompt_lengths, prompt_query=prompt_query, prompt_new=prompt_new, decode_query=decode_query, decode_new=decode_new, decode_cache=decode_cache, cached_lengths=cached_lengths)


def page_owners(prompt_lengths, page_count):
    end_pages = jnp.cumsum(prompt_lengths).astype(jnp.int32)
    page_ids = jnp.arange(page_count, dtype=jnp.int32)
    return lax.optimization_barrier(jnp.sum((page_ids[:, None] >= end_pages[None, :]).astype(jnp.int32), axis=1))

def softmax_parts(scores, own_score, is_live):
    masked = jnp.where(is_live, scores, -jnp.inf)
    top_score = jnp.maximum(lax.optimization_barrier(jnp.max(masked, axis=-1)), own_score)
    weights = jnp.where(is_live, jnp.exp(scores - top_score[..., None]), 0.0)
    own_weight = jnp.exp(own_score - top_score)
    denominator = lax.optimization_barrier(jnp.sum(weights, axis=-1)) + own_weight
    rounded = lax.optimization_barrier(weights.astype(jnp.bfloat16)).astype(jnp.float32)
    own_rounded = lax.optimization_barrier(own_weight.astype(jnp.bfloat16)).astype(jnp.float32)
    return (rounded, own_rounded, denominator)

def reference(prefill_kv, page_table, prompt_lengths, prompt_query, prompt_new, decode_query, decode_new, decode_cache, cached_lengths):
    scaling = 1.0 / math.sqrt(HD)
    group_size = QH // KVH
    page_count = prefill_kv.shape[0]
    page_owner = page_owners(prompt_lengths, page_count)
    kv_pool = jnp.zeros((POOL_DEV * N_ROW,) + prefill_kv.shape[1:], jnp.bfloat16).at[page_table].set(prefill_kv)
    key_rows = prefill_kv[:, :, 0].reshape(page_count * PAGE, KVH, HD).astype(jnp.float32)
    value_rows = prefill_kv[:, :, 1].reshape(page_count * PAGE, KVH, HD).astype(jnp.float32)
    token_owner = jnp.repeat(page_owner, PAGE)
    grouped = prompt_query.astype(jnp.float32).reshape(PROMPTS, KVH, group_size, HD)
    scores = jnp.einsum('jkgd,tkd->jkgt', grouped, key_rows) * scaling
    is_live = (token_owner[None, :] == jnp.arange(PROMPTS, dtype=jnp.int32)[:, None])[:, None, None, :]
    own_key = prompt_new[:, 0].astype(jnp.float32)
    own_value = prompt_new[:, 1].astype(jnp.float32)
    own_score = jnp.einsum('jkgd,jkd->jkg', grouped, own_key) * scaling
    weights, own_weight, denominator = softmax_parts(scores, own_score, is_live)
    numerator = jnp.einsum('jkgt,tkd->jkgd', weights, value_rows) + own_weight[..., None] * own_value[:, :, None, :]
    prompt_out = (numerator / denominator[..., None]).reshape(PROMPTS, QH * HD).astype(jnp.bfloat16)
    seq_count = decode_query.shape[0]
    dgrouped = decode_query.astype(jnp.float32).reshape(seq_count, KVH, group_size, HD)
    cache_keys = decode_cache[:, :, 0].astype(jnp.float32)
    cache_values = decode_cache[:, :, 1].astype(jnp.float32)
    dscores = jnp.einsum('skgd,stkd->skgt', dgrouped, cache_keys) * scaling
    dlive = (jnp.arange(CACHE, dtype=jnp.int32)[None, :] < cached_lengths[:, None])[:, None, None, :]
    down_key = decode_new[:, 0].astype(jnp.float32)
    down_value = decode_new[:, 1].astype(jnp.float32)
    down_score = jnp.einsum('skgd,skd->skg', dgrouped, down_key) * scaling
    dweights, down_weight, ddenominator = softmax_parts(dscores, down_score, dlive)
    dnumerator = jnp.einsum('skgt,stkd->skgd', dweights, cache_values) + down_weight[..., None] * down_value[:, :, None, :]
    decode_out = (dnumerator / ddenominator[..., None]).reshape(seq_count, QH * HD).astype(jnp.bfloat16)
    return (decode_out, prompt_out, kv_pool)
```

```python
import functools
import math

import jax
import jax.numpy as jnp
from jax import lax
from jax.experimental import pallas as pl
from jax.experimental.pallas import tpu as pltpu
from jax.sharding import PartitionSpec as P

MESH = pl.DeviceIdType.MESH
LOWEST = -1e30
FLOOR = -1e29
LANES = 128
CONTRACT_LAST = (((1,), (1,)), ((), ()))


def partner(me, count, step):
    if count & (count - 1):
        return lax.rem(me + step, count)
    place, bit = 0, 1
    while bit < count:
        here = (me // bit) % 2
        place = place + bit * ((1 - here) if step & bit else here)
        bit *= 2
    return place


def softmax_pass(query, blocks, scores_ref, scaling):
    rows = query.shape[0]
    lane = lax.broadcasted_iota(jnp.int32, (rows, LANES), 1)
    peak = jnp.full((rows, LANES), FLOOR, jnp.float32)
    for load, width, at, first, lo, hi in blocks:
        raw = lax.dot_general(query, load(), CONTRACT_LAST, preferred_element_type=jnp.float32)
        for part in range(width // LANES):
            column = lane + (first + part * LANES)
            live = (column >= lo) & (column < hi)
            here = raw[:, part * LANES : (part + 1) * LANES] * scaling
            here = jnp.where(live, here, LOWEST)
            scores_ref[:, pl.ds(at + part * LANES, LANES)] = here
            peak = jnp.maximum(peak, here)
    top = jnp.max(peak, axis=1, keepdims=True)
    total = jnp.zeros((rows, LANES), jnp.float32)
    accumulated = jnp.zeros((rows, LANES), jnp.float32)
    for load, width, at, first, lo, hi in blocks:
        parts = []
        for part in range(width // LANES):
            weight = jnp.exp(scores_ref[:, pl.ds(at + part * LANES, LANES)] - top)
            total = total + weight
            parts.append(pltpu.roll(weight, 2, 1).astype(jnp.bfloat16))
        accumulated = accumulated + jnp.dot(
            jnp.concatenate(parts, axis=1), load(), preferred_element_type=jnp.float32
        )
    return top, jnp.sum(total, axis=1, keepdims=True), accumulated


def kernel(
    count,
    scaling,
    source_ref,
    lengths_ref,
    cached_ref,
    pages_hbm,
    cache_hbm,
    query_ref,
    new_ref,
    decode_query_ref,
    decode_new_ref,
    decode_out_ref,
    prompt_out_ref,
    pool_ref,
    pages,
    cache,
    sections,
    own_rows,
    decode_own_rows,
    scores,
    decode_scores,
    staged,
    decode_staged,
    accs,
    stats,
    local_sem,
    send_sem,
    recv_sem,
    acc_send_sem,
    acc_recv_sem,
    stat_send_sem,
    stat_recv_sem,
):
    me = lax.axis_index("row")
    page_count, page_rows = pages.shape[0], pages.shape[1]
    per_pair = page_count // count
    heads = query_ref.shape[1]
    prompts = query_ref.shape[0]
    barrier = pltpu.get_barrier_semaphore()
    for step in range(1, count):
        pl.semaphore_signal(
            barrier, inc=1, device_id={"row": partner(me, count, step)}, device_id_type=MESH
        )
    pages_in = pltpu.make_async_copy(pages_hbm, pages, local_sem.at[0])
    pages_in.start()
    cache_in = pltpu.make_async_copy(cache_hbm, cache, local_sem.at[1])
    cache_in.start()

    def gather(place):
        def body(i, carry):
            slot = place * per_pair + i
            sections[slot] = pages[source_ref[slot]]
            return carry

        lax.fori_loop(0, per_pair, body, 0, unroll=min(8, per_pair))

    pages_in.wait()
    sends = []
    for step in reversed(range(1, count)):
        place = partner(me, count, step)
        gather(place)
        if step == count - 1:
            pl.semaphore_wait(barrier, count - 1)
        send = pltpu.make_async_remote_copy(
            src_ref=sections.at[pl.ds(place * per_pair, per_pair)],
            dst_ref=pool_ref.at[pl.ds(me * per_pair, per_pair)],
            send_sem=send_sem.at[step - 1],
            recv_sem=recv_sem.at[step - 1],
            device_id={"row": place},
            device_id_type=MESH,
        )
        send.start()
        sends.append(send)
    gather(me)
    kept = pltpu.make_async_copy(
        sections.at[pl.ds(me * per_pair, per_pair)],
        pool_ref.at[pl.ds(me * per_pair, per_pair)],
        local_sem.at[2],
    )
    kept.start()

    rows = prompts * heads
    row = lax.broadcasted_iota(jnp.int32, (rows, LANES), 0)
    lane = lax.broadcasted_iota(jnp.int32, (rows, LANES), 1)
    head_live = lane % 4 == (row // (heads // 2)) % 2
    far = jnp.int32(1 << 30)
    lo = jnp.zeros((rows, LANES), jnp.int32)
    hi = jnp.zeros((rows, LANES), jnp.int32)
    begin = -me * page_count
    for prompt in range(prompts):
        end = begin + lengths_ref[prompt]
        mine = row // heads == prompt
        lo = jnp.where(mine, begin * page_rows, lo)
        hi = jnp.where(mine, end * page_rows, hi)
        begin = end
    lo = jnp.where(head_live, lo, far)
    own_lo = jnp.where(head_live, (row // heads) * 4, far)
    own_hi = (row // heads) * 4 + 4
    own_lo = jnp.where(me == 0, own_lo, far)
    own_rows[...] = jnp.zeros_like(own_rows)
    own_rows[: new_ref.shape[0], :] = new_ref[...]
    query = query_ref[...].reshape(rows, LANES)
    chunk = 32
    blocks = [(lambda: own_rows[...], LANES, page_count * page_rows, 0, own_lo, own_hi)]
    for at in range(0, page_count, chunk):
        blocks.append(
            (
                lambda at=at: pages[at : at + chunk].reshape(chunk * page_rows, LANES),
                chunk * page_rows,
                at * page_rows,
                at * page_rows,
                lo,
                hi,
            )
        )
    top, total, accumulated = softmax_pass(query, blocks, scores, scaling)
    accs[me] = accumulated.astype(jnp.bfloat16)
    eye = row == lane

    def as_row(column):
        return jnp.sum(jnp.where(eye, column, 0.0), axis=0, keepdims=True)

    def as_column(line):
        return jnp.sum(jnp.where(eye, line, 0.0), axis=1, keepdims=True)

    stats[me] = jnp.concatenate(
        [as_row(top), as_row(total), jnp.zeros((6, LANES), jnp.float32)], axis=0
    )
    for step in reversed(range(1, count)):
        place = partner(me, count, step)
        for held, out_sem, in_sem in (
            (accs, acc_send_sem, acc_recv_sem),
            (stats, stat_send_sem, stat_recv_sem),
        ):
            send = pltpu.make_async_remote_copy(
                src_ref=held.at[me],
                dst_ref=held.at[me],
                send_sem=out_sem.at[step - 1],
                recv_sem=in_sem.at[step - 1],
                device_id={"row": place},
                device_id_type=MESH,
            )
            send.start()
            sends.append(send)

    seqs = decode_query_ref.shape[0]
    cache_rows = cache.shape[1]
    cache_in.wait()
    decode_own_rows[...] = jnp.zeros_like(decode_own_rows)
    decode_own_rows[: decode_new_ref.shape[0], :] = decode_new_ref[...].astype(jnp.float32)
    row = lax.broadcasted_iota(jnp.int32, (heads, LANES), 0)
    lane = lax.broadcasted_iota(jnp.int32, (heads, LANES), 1)
    head_live = lane % 4 == (row // (heads // 2)) % 2
    for seq in range(seqs):
        lo = jnp.where(head_live, 0, far)
        hi = jnp.full((heads, LANES), cached_ref[seq] * 4, jnp.int32)
        own_lo = jnp.where(head_live, seq * 4, far)
        own_hi = jnp.full((heads, LANES), seq * 4 + 4, jnp.int32)
        blocks = [
            (
                lambda: decode_own_rows[...].astype(jnp.bfloat16),
                LANES,
                cache_rows,
                0,
                own_lo,
                own_hi,
            ),
            (lambda seq=seq: cache[seq], cache_rows, 0, 0, lo, hi),
        ]
        top, total, accumulated = softmax_pass(
            decode_query_ref[seq], blocks, decode_scores, scaling
        )
        decode_staged[seq * heads : (seq + 1) * heads, :] = accumulated / total
    for head in range(heads):
        decode_out_ref[:, head * LANES : (head + 1) * LANES] = decode_staged[
            pl.ds(head, seqs, stride=heads), :
        ].astype(jnp.bfloat16)

    for send in sends[count - 1 :]:
        send.wait_recv()
    top = jnp.full((1, LANES), FLOOR, jnp.float32)
    for k in range(count):
        top = jnp.maximum(top, stats[k, 0:1, :])
    total = jnp.zeros((1, LANES), jnp.float32)
    for k in range(count):
        total = total + stats[k, 1:2, :] * jnp.exp(stats[k, 0:1, :] - top)
    joined = jnp.zeros((rows, LANES), jnp.float32)
    for k in range(count):
        share = as_column(jnp.exp(stats[k, 0:1, :] - top) / total)
        joined = joined + accs[k].astype(jnp.float32) * share
    staged[...] = joined
    for head in range(heads):
        prompt_out_ref[:, head * LANES : (head + 1) * LANES] = staged[
            pl.ds(head, prompts, stride=heads), :
        ].astype(jnp.bfloat16)

    kept.wait()
    for send in sends[: count - 1]:
        send.wait_recv()
    for send in sends:
        send.wait_send()


def per_device(
    prefill_kv,
    page_table,
    prompt_lengths,
    prompt_query,
    prompt_new,
    decode_query,
    decode_new,
    decode_cache,
    cached_lengths,
):
    count = lax.axis_size("row")
    page_count = prefill_kv.shape[0]
    head_depth = prefill_kv.shape[4]
    page_rows = math.prod(prefill_kv.shape[1:4])
    per_pair = page_count // count
    prompts, heads = prompt_query.shape[:2]
    seqs = decode_query.shape[0]
    cache_rows = math.prod(decode_cache.shape[1:4])
    target = page_table // page_count * per_pair + page_table % per_pair
    ids = jnp.arange(page_count, dtype=jnp.int32)
    source = jnp.sum(jnp.where(target[None, :] == ids[:, None], ids[None, :], 0), axis=1)
    smem = pl.BlockSpec(memory_space=pltpu.SMEM)
    vmem = pl.BlockSpec(memory_space=pltpu.VMEM)
    anywhere = pl.BlockSpec(memory_space=pl.ANY)
    decode_out, prompt_out, pool = pl.pallas_call(
        functools.partial(kernel, count, 1.0 / math.sqrt(head_depth)),
        out_shape=(
            jax.ShapeDtypeStruct((seqs, heads * head_depth), jnp.bfloat16),
            jax.ShapeDtypeStruct((prompts, heads * head_depth), jnp.bfloat16),
            jax.ShapeDtypeStruct((page_count, page_rows, head_depth), jnp.bfloat16),
        ),
        in_specs=[smem] * 3 + [anywhere] * 2 + [vmem] * 4,
        out_specs=(vmem, vmem, anywhere),
        scratch_shapes=[
            pltpu.VMEM((page_count, page_rows, head_depth), jnp.bfloat16),
            pltpu.VMEM((seqs, cache_rows, head_depth), jnp.bfloat16),
            pltpu.VMEM((page_count, page_rows, head_depth), jnp.bfloat16),
            pltpu.VMEM((LANES, head_depth), jnp.bfloat16),
            pltpu.VMEM((LANES, head_depth), jnp.float32),
            pltpu.VMEM((prompts * heads, page_count * page_rows + LANES), jnp.float32),
            pltpu.VMEM((heads, cache_rows + LANES), jnp.float32),
            pltpu.VMEM((prompts * heads, head_depth), jnp.float32),
            pltpu.VMEM((seqs * heads, head_depth), jnp.float32),
            pltpu.VMEM((count, prompts * heads, head_depth), jnp.bfloat16),
            pltpu.VMEM((count, 8, LANES), jnp.float32),
            pltpu.SemaphoreType.DMA((3,)),
            pltpu.SemaphoreType.DMA((count - 1,)),
            pltpu.SemaphoreType.DMA((count - 1,)),
            pltpu.SemaphoreType.DMA((count - 1,)),
            pltpu.SemaphoreType.DMA((count - 1,)),
            pltpu.SemaphoreType.DMA((count - 1,)),
            pltpu.SemaphoreType.DMA((count - 1,)),
        ],
        compiler_params=pltpu.CompilerParams(
            collective_id=0, has_side_effects=True, vmem_limit_bytes=32 * 1024 * 1024
        ),
    )(
        source,
        prompt_lengths,
        cached_lengths,
        prefill_kv.reshape(page_count, page_rows, head_depth),
        decode_cache.reshape(seqs, cache_rows, head_depth),
        prompt_query,
        prompt_new.reshape(-1, head_depth),
        decode_query,
        decode_new.reshape(-1, head_depth),
    )
    return decode_out, prompt_out, pool.reshape(prefill_kv.shape)


def solution(mesh):
    in_specs = (
        P(("grp", "row"), None, None, "head", None),
        P(("grp", "row")),
        P("grp"),
        P("grp", "head", None),
        P("grp", None, "head", None),
        P(("grp", "row"), "head", None),
        P(("grp", "row"), None, "head", None),
        P(("grp", "row"), None, None, "head", None),
        P(("grp", "row")),
    )
    out_specs = (
        P(("grp", "row"), "head"),
        P("grp", "head"),
        P(("grp", "row"), None, None, "head", None),
    )
    return jax.shard_map(
        per_device, mesh=mesh, in_specs=in_specs, out_specs=out_specs, check_vma=False
    )
```

```python
import functools
import math

import jax
import jax.numpy as jnp
from jax import lax
from jax.experimental import pallas as pl
from jax.experimental.pallas import tpu as pltpu
from jax.sharding import PartitionSpec as P

MESH = pl.DeviceIdType.MESH
LOWEST = -1e30
FLOOR = -1e29
LANES = 128
CONTRACT_LAST = (((1,), (1,)), ((), ()))


def partner(me, count, step):
    if count & (count - 1):
        return lax.rem(me + step, count)
    place, bit = 0, 1
    while bit < count:
        here = (me // bit) % 2
        place = place + bit * ((1 - here) if step & bit else here)
        bit *= 2
    return place


def softmax_pass(query, blocks, scores_ref, scaling):
    rows = query.shape[0]
    lane = lax.broadcasted_iota(jnp.int32, (rows, LANES), 1)
    peak = jnp.full((rows, LANES), FLOOR, jnp.float32)
    for load, width, at, first, lo, hi in blocks:
        raw = lax.dot_general(query, load(), CONTRACT_LAST, preferred_element_type=jnp.float32)
        for part in range(width // LANES):
            column = lane + (first + part * LANES)
            live = (column >= lo) & (column < hi)
            here = raw[:, part * LANES : (part + 1) * LANES] * scaling
            here = jnp.where(live, here, LOWEST)
            scores_ref[:, pl.ds(at + part * LANES, LANES)] = here
            peak = jnp.maximum(peak, here)
    top = jnp.max(peak, axis=1, keepdims=True)
    total = jnp.zeros((rows, LANES), jnp.float32)
    accumulated = jnp.zeros((rows, LANES), jnp.float32)
    for load, width, at, first, lo, hi in blocks:
        parts = []
        for part in range(width // LANES):
            weight = jnp.exp(scores_ref[:, pl.ds(at + part * LANES, LANES)] - top)
            total = total + weight
            parts.append(pltpu.roll(weight, 2, 1).astype(jnp.bfloat16))
        accumulated = accumulated + jnp.dot(
            jnp.concatenate(parts, axis=1), load(), preferred_element_type=jnp.float32
        )
    return top, jnp.sum(total, axis=1, keepdims=True), accumulated


def plan_phases(count, per_pair):
    pieces = 4 if per_pair % 4 == 0 else 1
    width = per_pair // pieces
    far_steps = [step for step in range(1, count) if step >= count // 2]
    near_steps = [step for step in range(1, count) if step < count // 2]
    far = [(step, piece * width, width) for piece in range(pieces) for step in far_steps]
    near = [(step, piece * width, width) for piece in range(pieces) for step in near_steps]
    f1, f2 = len(far) * 3 // 8, len(far) * 6 // 8
    n1, n2 = len(near) // 4, len(near) * 3 // 4
    return (far[:f1] + near[:n1], far[f1:f2] + near[n1:n2], far[f2:] + near[n2:])


def kernel(
    count,
    scaling,
    source_ref,
    lengths_ref,
    cached_ref,
    pages_hbm,
    cache_hbm,
    query_hbm,
    new_hbm,
    decode_query_hbm,
    decode_new_hbm,
    decode_out_ref,
    prompt_out_ref,
    pool_ref,
    pages,
    cache,
    query,
    new,
    decode_query,
    decode_new,
    sections,
    own_rows,
    decode_own_rows,
    scores,
    decode_scores,
    staged,
    decode_staged,
    outbox,
    inbox,
    gathered,
    local_sem,
    send_sem,
    recv_sem,
    part_send_sem,
    part_recv_sem,
    out_send_sem,
    out_recv_sem,
):
    me = lax.axis_index("row")
    page_count, page_rows = pages.shape[0], pages.shape[1]
    per_pair = page_count // count
    prompts, heads = query.shape[:2]
    rows = prompts * heads
    share = gathered.shape[1]
    split = share != rows
    barrier = pltpu.get_barrier_semaphore()
    for step in range(1, count):
        pl.semaphore_signal(
            barrier, inc=1, device_id={"row": partner(me, count, step)}, device_id_type=MESH
        )
    incoming = [
        pltpu.make_async_copy(there, here, local_sem.at[i])
        for i, (there, here) in enumerate(
            (
                (pages_hbm, pages),
                (query_hbm, query),
                (new_hbm, new),
                (cache_hbm, cache),
                (decode_query_hbm, decode_query),
                (decode_new_hbm, decode_new),
            )
        )
    ]
    for copy in incoming:
        copy.start()

    def gather(place, first, width):
        def body(i, carry):
            slot = place * per_pair + first + i
            sections[slot] = pages[source_ref[slot]]
            return carry

        lax.fori_loop(0, width, body, 0, unroll=min(8, width))

    page_sends = []

    def send_pages(phase):
        for step, first, width in phase:
            place = partner(me, count, step)
            at = len(page_sends)
            send = pltpu.make_async_remote_copy(
                src_ref=sections.at[pl.ds(place * per_pair + first, width)],
                dst_ref=pool_ref.at[pl.ds(me * per_pair + first, width)],
                send_sem=send_sem.at[at],
                recv_sem=recv_sem.at[at],
                device_id={"row": place},
                device_id_type=MESH,
            )
            send.start()
            page_sends.append(send)

    def exchange(source, target, out_sem, in_sem):
        sends = []
        for step in reversed(range(1, count)):
            place = partner(me, count, step)
            send = pltpu.make_async_remote_copy(
                src_ref=source(place),
                dst_ref=target,
                send_sem=out_sem.at[step - 1],
                recv_sem=in_sem.at[step - 1],
                device_id={"row": place},
                device_id_type=MESH,
            )
            send.start()
            sends.append(send)
        return sends

    phases = plan_phases(count, per_pair)
    incoming[0].wait()
    for step, first, width in phases[0]:
        gather(partner(me, count, step), first, width)
    pl.semaphore_wait(barrier, count - 1)
    send_pages(phases[0])
    for step, first, width in phases[1] + phases[2]:
        gather(partner(me, count, step), first, width)
    gather(me, 0, per_pair)
    kept = pltpu.make_async_copy(
        sections.at[pl.ds(me * per_pair, per_pair)],
        pool_ref.at[pl.ds(me * per_pair, per_pair)],
        local_sem.at[6],
    )
    kept.start()

    row = lax.broadcasted_iota(jnp.int32, (rows, LANES), 0)
    lane = lax.broadcasted_iota(jnp.int32, (rows, LANES), 1)
    head_live = lane % 4 == (row // (heads // 2)) % 2
    far = jnp.int32(1 << 30)
    lo = jnp.zeros((rows, LANES), jnp.int32)
    hi = jnp.zeros((rows, LANES), jnp.int32)
    begin = -me * page_count
    for prompt in range(prompts):
        end = begin + lengths_ref[prompt]
        mine = row // heads == prompt
        lo = jnp.where(mine, begin * page_rows, lo)
        hi = jnp.where(mine, end * page_rows, hi)
        begin = end
    lo = jnp.where(head_live, lo, far)
    own_lo = jnp.where(head_live, (row // heads) * 4, far)
    own_hi = (row // heads) * 4 + 4
    own_lo = jnp.where(me == 0, own_lo, far)
    incoming[1].wait()
    incoming[2].wait()
    own_rows[...] = jnp.zeros_like(own_rows)
    own_rows[: new.shape[0], :] = new[...]
    chunk = 32
    blocks = [(lambda: own_rows[...], LANES, page_count * page_rows, 0, own_lo, own_hi)]
    for at in range(0, page_count, chunk):
        blocks.append(
            (
                lambda at=at: pages[at : at + chunk].reshape(chunk * page_rows, LANES),
                chunk * page_rows,
                at * page_rows,
                at * page_rows,
                lo,
                hi,
            )
        )
    top, total, accumulated = softmax_pass(
        query[...].reshape(rows, LANES), blocks, scores, scaling
    )
    eye = row == lane
    stats = jnp.concatenate(
        [
            jnp.sum(jnp.where(eye, top, 0.0), axis=0, keepdims=True),
            jnp.sum(jnp.where(eye, total, 0.0), axis=0, keepdims=True),
            jnp.zeros((6, LANES), jnp.float32),
        ],
        axis=0,
    )
    for k in range(rows // share):
        outbox[k, :share, :] = accumulated[k * share : (k + 1) * share, :]
        outbox[k, share:, :] = stats
    inbox[me] = outbox[me if split else 0]
    part_sends = exchange(
        lambda place: outbox.at[place if split else 0], inbox.at[me], part_send_sem, part_recv_sem
    )
    send_pages(phases[1])

    seqs = decode_query.shape[0]
    cache_rows = cache.shape[1]
    for copy in incoming[3:]:
        copy.wait()
    decode_own_rows[...] = jnp.zeros_like(decode_own_rows)
    for seq in range(seqs):
        for kind in range(2):
            at = seq * 4 + kind * 2
            decode_own_rows[at : at + 2, :] = decode_new[seq, kind].astype(jnp.float32)
    row = lax.broadcasted_iota(jnp.int32, (heads, LANES), 0)
    lane = lax.broadcasted_iota(jnp.int32, (heads, LANES), 1)
    head_live = lane % 4 == (row // (heads // 2)) % 2
    for seq in range(seqs):
        lo = jnp.where(head_live, 0, far)
        hi = jnp.full((heads, LANES), cached_ref[seq] * 4, jnp.int32)
        own_lo = jnp.where(head_live, seq * 4, far)
        own_hi = jnp.full((heads, LANES), seq * 4 + 4, jnp.int32)
        blocks = [
            (
                lambda: decode_own_rows[...].astype(jnp.bfloat16),
                LANES,
                cache_rows,
                0,
                own_lo,
                own_hi,
            ),
            (lambda seq=seq: cache[seq], cache_rows, 0, 0, lo, hi),
        ]
        top, total, accumulated = softmax_pass(decode_query[seq], blocks, decode_scores, scaling)
        decode_staged[seq * heads : (seq + 1) * heads, :] = accumulated / total
    for head in range(heads):
        decode_out_ref[:, head * LANES : (head + 1) * LANES] = decode_staged[
            pl.ds(head, seqs, stride=heads), :
        ].astype(jnp.bfloat16)

    for send in part_sends:
        send.wait_recv()
    base = me * share if split else 0
    row = lax.broadcasted_iota(jnp.int32, (share, LANES), 0)
    lane = lax.broadcasted_iota(jnp.int32, (share, LANES), 1)
    eye = row + base == lane
    top = jnp.full((1, LANES), FLOOR, jnp.float32)
    for k in range(count):
        top = jnp.maximum(top, inbox[k, share : share + 1, :])
    total = jnp.zeros((1, LANES), jnp.float32)
    for k in range(count):
        total = total + inbox[k, share + 1 : share + 2, :] * jnp.exp(
            inbox[k, share : share + 1, :] - top
        )
    joined = jnp.zeros((share, LANES), jnp.float32)
    for k in range(count):
        weight = jnp.exp(inbox[k, share : share + 1, :] - top) / total
        weight = jnp.sum(jnp.where(eye, weight, 0.0), axis=1, keepdims=True)
        joined = joined + inbox[k, :share, :] * weight
    gathered[me if split else 0] = joined.astype(jnp.bfloat16)
    out_sends = []
    if split:
        out_sends = exchange(
            lambda place: gathered.at[me], gathered.at[me], out_send_sem, out_recv_sem
        )
    send_pages(phases[2])
    for send in out_sends:
        send.wait_recv()
    for k in range(rows // share):
        staged[k * share : (k + 1) * share, :] = gathered[k].astype(jnp.float32)
    for head in range(heads):
        prompt_out_ref[:, head * LANES : (head + 1) * LANES] = staged[
            pl.ds(head, prompts, stride=heads), :
        ].astype(jnp.bfloat16)

    kept.wait()
    for send in page_sends:
        send.wait_recv()
    for send in part_sends + out_sends + page_sends:
        send.wait_send()


def write_out(first, second, third, first_out, second_out, third_out, sem):
    copies = [
        pltpu.make_async_copy(here, there, sem.at[i])
        for i, (here, there) in enumerate(
            ((third, third_out), (second, second_out), (first, first_out))
        )
    ]
    for copy in copies:
        copy.start()
    for copy in copies:
        copy.wait()


def per_device(
    prefill_kv,
    page_table,
    prompt_lengths,
    prompt_query,
    prompt_new,
    decode_query,
    decode_new,
    decode_cache,
    cached_lengths,
):
    count = lax.axis_size("row")
    page_count = prefill_kv.shape[0]
    head_depth = prefill_kv.shape[4]
    page_rows = math.prod(prefill_kv.shape[1:4])
    per_pair = page_count // count
    prompts, heads = prompt_query.shape[:2]
    rows = prompts * heads
    share = rows // count if rows % (16 * count) == 0 else rows
    seqs = decode_query.shape[0]
    cache_rows = math.prod(decode_cache.shape[1:4])
    messages = sum(len(phase) for phase in plan_phases(count, per_pair))
    target = page_table // page_count * per_pair + page_table % per_pair
    ids = jnp.arange(page_count, dtype=jnp.int32)
    source = jnp.sum(jnp.where(target[None, :] == ids[:, None], ids[None, :], 0), axis=1)
    smem = pl.BlockSpec(memory_space=pltpu.SMEM)
    vmem = pl.BlockSpec(memory_space=pltpu.VMEM)
    hbm = pl.BlockSpec(memory_space=pltpu.HBM)
    anywhere = pl.BlockSpec(memory_space=pl.ANY)
    bf16, f32 = jnp.bfloat16, jnp.float32
    out_shape = (
        jax.ShapeDtypeStruct((seqs, heads * head_depth), bf16),
        jax.ShapeDtypeStruct((prompts, heads * head_depth), bf16),
        jax.ShapeDtypeStruct((page_count, page_rows, head_depth), bf16),
    )
    vmem_shape = (
        pltpu.VMEM((seqs, heads * head_depth), bf16),
        pltpu.VMEM((prompts, heads * head_depth), bf16),
        pltpu.VMEM((page_count, page_rows, head_depth), bf16),
    )
    results = pl.pallas_call(
        functools.partial(kernel, count, 1.0 / math.sqrt(head_depth)),
        out_shape=vmem_shape,
        in_specs=[smem] * 3 + [hbm] * 6,
        out_specs=(vmem, vmem, vmem),
        scratch_shapes=[
            pltpu.VMEM((page_count, page_rows, head_depth), bf16),
            pltpu.VMEM((seqs, cache_rows, head_depth), bf16),
            pltpu.VMEM(prompt_query.shape, bf16),
            pltpu.VMEM((prompts * 4, head_depth), bf16),
            pltpu.VMEM(decode_query.shape, bf16),
            pltpu.VMEM(decode_new.shape, bf16),
            pltpu.VMEM((page_count, page_rows, head_depth), bf16),
            pltpu.VMEM((LANES, head_depth), bf16),
            pltpu.VMEM((LANES, head_depth), f32),
            pltpu.VMEM((rows, page_count * page_rows + LANES), f32),
            pltpu.VMEM((heads, cache_rows + LANES), f32),
            pltpu.VMEM((rows, head_depth), f32),
            pltpu.VMEM((seqs * heads, head_depth), f32),
            pltpu.VMEM((rows // share, share + 8, LANES), f32),
            pltpu.VMEM((count, share + 8, LANES), f32),
            pltpu.VMEM((rows // share, share, LANES), bf16),
            pltpu.SemaphoreType.DMA((7,)),
            pltpu.SemaphoreType.DMA((messages,)),
            pltpu.SemaphoreType.DMA((messages,)),
            pltpu.SemaphoreType.DMA((count - 1,)),
            pltpu.SemaphoreType.DMA((count - 1,)),
            pltpu.SemaphoreType.DMA((count - 1,)),
            pltpu.SemaphoreType.DMA((count - 1,)),
        ],
        compiler_params=pltpu.CompilerParams(
            collective_id=0, has_side_effects=True, vmem_limit_bytes=58 * 1024 * 1024
        ),
    )(
        source,
        prompt_lengths,
        cached_lengths,
        prefill_kv.reshape(page_count, page_rows, head_depth),
        decode_cache.reshape(seqs, cache_rows, head_depth),
        prompt_query,
        prompt_new.reshape(-1, head_depth),
        decode_query,
        decode_new,
    )
    decode_out, prompt_out, pool = pl.pallas_call(
        write_out,
        out_shape=out_shape,
        in_specs=[vmem] * 3,
        out_specs=(hbm,) * 3,
        scratch_shapes=[pltpu.SemaphoreType.DMA((3,))],
    )(*(pltpu.with_memory_space_constraint(x, pltpu.VMEM) for x in results))
    return decode_out, prompt_out, pool.reshape(prefill_kv.shape)


def solution(mesh):
    in_specs = (
        P(("grp", "row"), None, None, "head", None),
        P(("grp", "row")),
        P("grp"),
        P("grp", "head", None),
        P("grp", None, "head", None),
        P(("grp", "row"), "head", None),
        P(("grp", "row"), None, "head", None),
        P(("grp", "row"), None, None, "head", None),
        P(("grp", "row")),
    )
    out_specs = (
        P(("grp", "row"), "head"),
        P("grp", "head"),
        P(("grp", "row"), None, None, "head", None),
    )
    return jax.shard_map(
        per_device, mesh=mesh, in_specs=in_specs, out_specs=out_specs, check_vma=False
    )
```

```python
import functools
import math

import jax
import jax.numpy as jnp
from jax import lax
from jax.experimental import pallas as pl
from jax.experimental.pallas import tpu as pltpu
from jax.sharding import PartitionSpec as P

MESH = pl.DeviceIdType.MESH
LOWEST = -1e30
FLOOR = -1e29
LANES = 128
CONTRACT_LAST = (((1,), (1,)), ((), ()))


def partner(me, count, step):
    if count & (count - 1):
        return lax.rem(me + step, count)
    place, bit = 0, 1
    while bit < count:
        here = (me // bit) % 2
        place = place + bit * ((1 - here) if step & bit else here)
        bit *= 2
    return place


def softmax_pass(query, blocks, scores_ref, scaling):
    rows = query.shape[0]
    lane = lax.broadcasted_iota(jnp.int32, (rows, LANES), 1)
    peak = jnp.full((rows, LANES), FLOOR, jnp.float32)
    for load, width, at, first, lo, hi in blocks:
        raw = lax.dot_general(query, load(), CONTRACT_LAST, preferred_element_type=jnp.float32)
        for part in range(width // LANES):
            column = lane + (first + part * LANES)
            live = (column >= lo) & (column < hi)
            here = raw[:, part * LANES : (part + 1) * LANES] * scaling
            here = jnp.where(live, here, LOWEST)
            scores_ref[:, pl.ds(at + part * LANES, LANES)] = here
            peak = jnp.maximum(peak, here)
    top = jnp.max(peak, axis=1, keepdims=True)
    total = jnp.zeros((rows, LANES), jnp.float32)
    accumulated = jnp.zeros((rows, LANES), jnp.float32)
    for load, width, at, first, lo, hi in blocks:
        parts = []
        for part in range(width // LANES):
            weight = jnp.exp(scores_ref[:, pl.ds(at + part * LANES, LANES)] - top)
            total = total + weight
            parts.append(pltpu.roll(weight, 2, 1).astype(jnp.bfloat16))
        accumulated = accumulated + jnp.dot(
            jnp.concatenate(parts, axis=1), load(), preferred_element_type=jnp.float32
        )
    return top, jnp.sum(total, axis=1, keepdims=True), accumulated


def plan_phases(count, per_pair):
    pieces = 4 if per_pair % 4 == 0 else 1
    width = per_pair // pieces
    far_steps = [step for step in range(1, count) if step >= count // 2]
    near_steps = [step for step in range(1, count) if step < count // 2]
    far = [(step, piece * width, width) for piece in range(pieces) for step in far_steps]
    near = [(step, piece * width, width) for piece in range(pieces) for step in near_steps]
    f1, f2 = len(far) * 3 // 8, len(far) * 6 // 8
    n1, n2 = len(near) // 4, len(near) * 3 // 4
    return (far[:f1] + near[:n1], far[f1:f2] + near[n1:n2], far[f2:] + near[n2:])


def kernel(
    count,
    scaling,
    table_hbm,
    lengths_hbm,
    cached_hbm,
    pages_hbm,
    cache_hbm,
    query_hbm,
    new_hbm,
    decode_query_hbm,
    decode_new_hbm,
    decode_out_ref,
    prompt_out_ref,
    pool_ref,
    table,
    source,
    source_ref,
    lengths_ref,
    cached_ref,
    pages,
    cache,
    query,
    new,
    decode_query,
    decode_new,
    sections,
    own_rows,
    decode_own_rows,
    scores,
    decode_scores,
    staged,
    decode_staged,
    outbox,
    inbox,
    gathered,
    local_sem,
    send_sem,
    recv_sem,
    part_send_sem,
    part_recv_sem,
    out_send_sem,
    out_recv_sem,
):
    me = lax.axis_index("row")
    page_count, page_rows = pages.shape[0], pages.shape[1]
    per_pair = page_count // count
    prompts, heads = query.shape[:2]
    rows = prompts * heads
    share = gathered.shape[1]
    split = share != rows
    barrier = pltpu.get_barrier_semaphore()
    for step in range(1, count):
        pl.semaphore_signal(
            barrier, inc=1, device_id={"row": partner(me, count, step)}, device_id_type=MESH
        )
    incoming = [
        pltpu.make_async_copy(there, here, local_sem.at[i])
        for i, (there, here) in enumerate(
            (
                (table_hbm, table),
                (pages_hbm, pages),
                (lengths_hbm, lengths_ref),
                (cached_hbm, cached_ref),
                (query_hbm, query),
                (new_hbm, new),
                (cache_hbm, cache),
                (decode_query_hbm, decode_query),
                (decode_new_hbm, decode_new),
            )
        )
    ]
    for copy in incoming:
        copy.start()

    def gather(place, first, width):
        def body(i, carry):
            slot = place * per_pair + first + i
            sections[slot] = pages[source_ref[0, slot]]
            return carry

        lax.fori_loop(0, width, body, 0, unroll=min(8, width))

    page_sends = []

    def send_pages(phase):
        for step, first, width in phase:
            place = partner(me, count, step)
            at = len(page_sends)
            send = pltpu.make_async_remote_copy(
                src_ref=sections.at[pl.ds(place * per_pair + first, width)],
                dst_ref=pool_ref.at[pl.ds(me * per_pair + first, width)],
                send_sem=send_sem.at[at],
                recv_sem=recv_sem.at[at],
                device_id={"row": place},
                device_id_type=MESH,
            )
            send.start()
            page_sends.append(send)

    def exchange(source, target, out_sem, in_sem):
        sends = []
        for step in reversed(range(1, count)):
            place = partner(me, count, step)
            send = pltpu.make_async_remote_copy(
                src_ref=source(place),
                dst_ref=target,
                send_sem=out_sem.at[step - 1],
                recv_sem=in_sem.at[step - 1],
                device_id={"row": place},
                device_id_type=MESH,
            )
            send.start()
            sends.append(send)
        return sends

    phases = plan_phases(count, per_pair)
    incoming[0].wait()
    page = lax.broadcasted_iota(jnp.int32, (page_count, page_count), 0)
    slot = lax.broadcasted_iota(jnp.int32, (page_count, page_count), 1)
    entry = table[...]
    target = lax.div(entry, page_count) * per_pair + lax.rem(entry, per_pair)
    target = jnp.sum(jnp.where(page == slot, target, 0), axis=1, keepdims=True)
    source[...] = jnp.max(jnp.where(target == slot, page, 0), axis=0, keepdims=True)
    listed = pltpu.make_async_copy(source, source_ref, local_sem.at[10])
    listed.start()
    listed.wait()
    incoming[1].wait()
    for at, item in enumerate(phases[0]):
        step, first, width = item
        gather(partner(me, count, step), first, width)
        if at == 0:
            pl.semaphore_wait(barrier, count - 1)
        send_pages([item])
    for step, first, width in phases[1] + phases[2]:
        gather(partner(me, count, step), first, width)
    gather(me, 0, per_pair)
    kept = pltpu.make_async_copy(
        sections.at[pl.ds(me * per_pair, per_pair)],
        pool_ref.at[pl.ds(me * per_pair, per_pair)],
        local_sem.at[9],
    )
    kept.start()

    row = lax.broadcasted_iota(jnp.int32, (rows, LANES), 0)
    lane = lax.broadcasted_iota(jnp.int32, (rows, LANES), 1)
    head_live = lane % 4 == (row // (heads // 2)) % 2
    far = jnp.int32(1 << 30)
    lo = jnp.zeros((rows, LANES), jnp.int32)
    hi = jnp.zeros((rows, LANES), jnp.int32)
    incoming[2].wait()
    incoming[3].wait()
    begin = -me * page_count
    for prompt in range(prompts):
        end = begin + lengths_ref[prompt]
        mine = row // heads == prompt
        lo = jnp.where(mine, begin * page_rows, lo)
        hi = jnp.where(mine, end * page_rows, hi)
        begin = end
    lo = jnp.where(head_live, lo, far)
    own_lo = jnp.where(head_live, (row // heads) * 4, far)
    own_hi = (row // heads) * 4 + 4
    own_lo = jnp.where(me == 0, own_lo, far)
    incoming[4].wait()
    incoming[5].wait()
    own_rows[...] = jnp.zeros_like(own_rows)
    own_rows[: new.shape[0], :] = new[...]
    chunk = 32
    blocks = [(lambda: own_rows[...], LANES, page_count * page_rows, 0, own_lo, own_hi)]
    for at in range(0, page_count, chunk):
        blocks.append(
            (
                lambda at=at: pages[at : at + chunk].reshape(chunk * page_rows, LANES),
                chunk * page_rows,
                at * page_rows,
                at * page_rows,
                lo,
                hi,
            )
        )
    top, total, accumulated = softmax_pass(
        query[...].reshape(rows, LANES), blocks, scores, scaling
    )
    eye = row == lane
    stats = jnp.concatenate(
        [
            jnp.sum(jnp.where(eye, top, 0.0), axis=0, keepdims=True),
            jnp.sum(jnp.where(eye, total, 0.0), axis=0, keepdims=True),
            jnp.zeros((6, LANES), jnp.float32),
        ],
        axis=0,
    )
    for k in range(rows // share):
        outbox[k, :share, :] = accumulated[k * share : (k + 1) * share, :]
        outbox[k, share:, :] = stats
    inbox[me] = outbox[me if split else 0]
    part_sends = exchange(
        lambda place: outbox.at[place if split else 0, pl.ds(0, share + 2)],
        inbox.at[me, pl.ds(0, share + 2)],
        part_send_sem,
        part_recv_sem,
    )
    send_pages(phases[1])

    seqs = decode_query.shape[0]
    cache_rows = cache.shape[1]
    for copy in incoming[6:]:
        copy.wait()
    decode_own_rows[...] = jnp.zeros_like(decode_own_rows)
    for seq in range(seqs):
        for kind in range(2):
            at = seq * 4 + kind * 2
            decode_own_rows[at : at + 2, :] = decode_new[seq, kind].astype(jnp.float32)
    row = lax.broadcasted_iota(jnp.int32, (heads, LANES), 0)
    lane = lax.broadcasted_iota(jnp.int32, (heads, LANES), 1)
    head_live = lane % 4 == (row // (heads // 2)) % 2
    for seq in range(seqs):
        lo = jnp.where(head_live, 0, far)
        hi = jnp.full((heads, LANES), cached_ref[seq] * 4, jnp.int32)
        own_lo = jnp.where(head_live, seq * 4, far)
        own_hi = jnp.full((heads, LANES), seq * 4 + 4, jnp.int32)
        blocks = [
            (
                lambda: decode_own_rows[...].astype(jnp.bfloat16),
                LANES,
                cache_rows,
                0,
                own_lo,
                own_hi,
            ),
            (lambda seq=seq: cache[seq], cache_rows, 0, 0, lo, hi),
        ]
        top, total, accumulated = softmax_pass(decode_query[seq], blocks, decode_scores, scaling)
        decode_staged[seq * heads : (seq + 1) * heads, :] = accumulated / total
    for head in range(heads):
        decode_out_ref[:, head * LANES : (head + 1) * LANES] = decode_staged[
            pl.ds(head, seqs, stride=heads), :
        ].astype(jnp.bfloat16)

    for send in part_sends:
        send.wait_recv()
    base = me * share if split else 0
    row = lax.broadcasted_iota(jnp.int32, (share, LANES), 0)
    lane = lax.broadcasted_iota(jnp.int32, (share, LANES), 1)
    eye = row + base == lane
    top = jnp.full((1, LANES), FLOOR, jnp.float32)
    for k in range(count):
        top = jnp.maximum(top, inbox[k, share : share + 1, :])
    total = jnp.zeros((1, LANES), jnp.float32)
    for k in range(count):
        total = total + inbox[k, share + 1 : share + 2, :] * jnp.exp(
            inbox[k, share : share + 1, :] - top
        )
    joined = jnp.zeros((share, LANES), jnp.float32)
    for k in range(count):
        weight = jnp.exp(inbox[k, share : share + 1, :] - top) / total
        weight = jnp.sum(jnp.where(eye, weight, 0.0), axis=1, keepdims=True)
        joined = joined + inbox[k, :share, :] * weight
    gathered[me if split else 0] = joined.astype(jnp.bfloat16)
    out_sends = []
    if split:
        out_sends = exchange(
            lambda place: gathered.at[me], gathered.at[me], out_send_sem, out_recv_sem
        )
    send_pages(phases[2])
    for send in out_sends:
        send.wait_recv()
    for k in range(rows // share):
        staged[k * share : (k + 1) * share, :] = gathered[k].astype(jnp.float32)
    for head in range(heads):
        prompt_out_ref[:, head * LANES : (head + 1) * LANES] = staged[
            pl.ds(head, prompts, stride=heads), :
        ].astype(jnp.bfloat16)

    kept.wait()
    for send in page_sends:
        send.wait_recv()
    for send in part_sends + out_sends + page_sends:
        send.wait_send()


def write_out(first, second, third, first_out, second_out, third_out, sem):
    copies = [
        pltpu.make_async_copy(here, there, sem.at[i])
        for i, (here, there) in enumerate(
            ((third, third_out), (second, second_out), (first, first_out))
        )
    ]
    for copy in copies:
        copy.start()
    for copy in copies:
        copy.wait()


def per_device(
    prefill_kv,
    page_table,
    prompt_lengths,
    prompt_query,
    prompt_new,
    decode_query,
    decode_new,
    decode_cache,
    cached_lengths,
):
    count = lax.axis_size("row")
    page_count = prefill_kv.shape[0]
    head_depth = prefill_kv.shape[4]
    page_rows = math.prod(prefill_kv.shape[1:4])
    per_pair = page_count // count
    prompts, heads = prompt_query.shape[:2]
    rows = prompts * heads
    share = rows // count if rows % (16 * count) == 0 else rows
    seqs = decode_query.shape[0]
    cache_rows = math.prod(decode_cache.shape[1:4])
    messages = sum(len(phase) for phase in plan_phases(count, per_pair))
    vmem = pl.BlockSpec(memory_space=pltpu.VMEM)
    hbm = pl.BlockSpec(memory_space=pltpu.HBM)
    anywhere = pl.BlockSpec(memory_space=pl.ANY)
    bf16, f32 = jnp.bfloat16, jnp.float32
    out_shape = (
        jax.ShapeDtypeStruct((seqs, heads * head_depth), bf16),
        jax.ShapeDtypeStruct((prompts, heads * head_depth), bf16),
        jax.ShapeDtypeStruct((page_count, page_rows, head_depth), bf16),
    )
    vmem_shape = (
        pltpu.VMEM((seqs, heads * head_depth), bf16),
        pltpu.VMEM((prompts, heads * head_depth), bf16),
        pltpu.VMEM((page_count, page_rows, head_depth), bf16),
    )
    results = pl.pallas_call(
        functools.partial(kernel, count, 1.0 / math.sqrt(head_depth)),
        out_shape=vmem_shape,
        in_specs=[hbm] * 9,
        out_specs=(vmem, vmem, vmem),
        scratch_shapes=[
            pltpu.VMEM((1, page_count), jnp.int32),
            pltpu.VMEM((1, page_count), jnp.int32),
            pltpu.SMEM((1, page_count), jnp.int32),
            pltpu.SMEM(prompt_lengths.shape, jnp.int32),
            pltpu.SMEM(cached_lengths.shape, jnp.int32),
            pltpu.VMEM((page_count, page_rows, head_depth), bf16),
            pltpu.VMEM((seqs, cache_rows, head_depth), bf16),
            pltpu.VMEM(prompt_query.shape, bf16),
            pltpu.VMEM((prompts * 4, head_depth), bf16),
            pltpu.VMEM(decode_query.shape, bf16),
            pltpu.VMEM(decode_new.shape, bf16),
            pltpu.VMEM((page_count, page_rows, head_depth), bf16),
            pltpu.VMEM((LANES, head_depth), bf16),
            pltpu.VMEM((LANES, head_depth), f32),
            pltpu.VMEM((rows, page_count * page_rows + LANES), f32),
            pltpu.VMEM((heads, cache_rows + LANES), f32),
            pltpu.VMEM((rows, head_depth), f32),
            pltpu.VMEM((seqs * heads, head_depth), f32),
            pltpu.VMEM((rows // share, share + 8, LANES), f32),
            pltpu.VMEM((count, share + 8, LANES), f32),
            pltpu.VMEM((rows // share, share, LANES), bf16),
            pltpu.SemaphoreType.DMA((11,)),
            pltpu.SemaphoreType.DMA((messages,)),
            pltpu.SemaphoreType.DMA((messages,)),
            pltpu.SemaphoreType.DMA((count - 1,)),
            pltpu.SemaphoreType.DMA((count - 1,)),
            pltpu.SemaphoreType.DMA((count - 1,)),
            pltpu.SemaphoreType.DMA((count - 1,)),
        ],
        compiler_params=pltpu.CompilerParams(
            collective_id=0, has_side_effects=True, vmem_limit_bytes=58 * 1024 * 1024
        ),
    )(
        page_table.reshape(1, page_count),
        prompt_lengths,
        cached_lengths,
        prefill_kv.reshape(page_count, page_rows, head_depth),
        decode_cache.reshape(seqs, cache_rows, head_depth),
        prompt_query,
        prompt_new.reshape(-1, head_depth),
        decode_query,
        decode_new,
    )
    decode_out, prompt_out, pool = pl.pallas_call(
        write_out,
        out_shape=out_shape,
        in_specs=[vmem] * 3,
        out_specs=(hbm,) * 3,
        scratch_shapes=[pltpu.SemaphoreType.DMA((3,))],
    )(*(pltpu.with_memory_space_constraint(x, pltpu.VMEM) for x in results))
    return decode_out, prompt_out, pool.reshape(prefill_kv.shape)


def solution(mesh):
    in_specs = (
        P(("grp", "row"), None, None, "head", None),
        P(("grp", "row")),
        P("grp"),
        P("grp", "head", None),
        P("grp", None, "head", None),
        P(("grp", "row"), "head", None),
        P(("grp", "row"), None, "head", None),
        P(("grp", "row"), None, None, "head", None),
        P(("grp", "row")),
    )
    out_specs = (
        P(("grp", "row"), "head"),
        P("grp", "head"),
        P(("grp", "row"), None, None, "head", None),
    )
    return jax.shard_map(
        per_device, mesh=mesh, in_specs=in_specs, out_specs=out_specs, check_vma=False
    )
```

```python
import functools
import math

import jax
import jax.numpy as jnp
from jax import lax
from jax.experimental import pallas as pl
from jax.experimental.pallas import tpu as pltpu
from jax.sharding import PartitionSpec as P

MESH = pl.DeviceIdType.MESH
LOWEST = -1e30
FLOOR = -1e29
LANES = 128
CONTRACT_LAST = (((1,), (1,)), ((), ()))


def partner(me, count, step):
    if count & (count - 1):
        return lax.rem(me + step, count)
    place, bit = 0, 1
    while bit < count:
        here = (me // bit) % 2
        place = place + bit * ((1 - here) if step & bit else here)
        bit *= 2
    return place


def softmax_pass(query, blocks, scores_ref, scaling):
    rows = query.shape[0]
    lane = lax.broadcasted_iota(jnp.int32, (rows, LANES), 1)
    peak = jnp.full((rows, LANES), FLOOR, jnp.float32)
    for load, width, at, first, lo, hi in blocks:
        raw = lax.dot_general(query, load(), CONTRACT_LAST, preferred_element_type=jnp.float32)
        for part in range(width // LANES):
            column = lane + (first + part * LANES)
            live = (column >= lo) & (column < hi)
            here = raw[:, part * LANES : (part + 1) * LANES] * scaling
            here = jnp.where(live, here, LOWEST)
            scores_ref[:, pl.ds(at + part * LANES, LANES)] = here
            peak = jnp.maximum(peak, here)
    top = jnp.max(peak, axis=1, keepdims=True)
    total = jnp.zeros((rows, LANES), jnp.float32)
    accumulated = jnp.zeros((rows, LANES), jnp.float32)
    for load, width, at, first, lo, hi in blocks:
        parts = []
        for part in range(width // LANES):
            weight = jnp.exp(scores_ref[:, pl.ds(at + part * LANES, LANES)] - top)
            total = total + weight
            parts.append(pltpu.roll(weight, 2, 1).astype(jnp.bfloat16))
        accumulated = accumulated + jnp.dot(
            jnp.concatenate(parts, axis=1), load(), preferred_element_type=jnp.float32
        )
    return top, jnp.sum(total, axis=1, keepdims=True), accumulated


def plan_phases(count, per_pair):
    pieces = 2 if per_pair % 2 == 0 else 1
    width = per_pair // pieces
    far_steps = [step for step in range(1, count) if step >= count // 2]
    near_steps = [step for step in range(1, count) if step < count // 2]
    far = [(step, piece * width, width) for piece in range(pieces) for step in far_steps]
    near = [(step, piece * width, width) for piece in range(pieces) for step in near_steps]
    f1, f2 = len(far) * 4 // 8, len(far) * 6 // 8
    n1, n2 = len(near) * 2 // 4, len(near) * 4 // 4
    return (far[:f1] + near[:n1], far[f1:f2] + near[n1:n2], far[f2:] + near[n2:])


def kernel(
    count,
    scaling,
    table_hbm,
    lengths_hbm,
    cached_hbm,
    pages_hbm,
    cache_hbm,
    query_hbm,
    new_hbm,
    decode_query_hbm,
    decode_new_hbm,
    decode_out_ref,
    prompt_out_ref,
    pool_ref,
    table,
    source,
    source_ref,
    lengths_ref,
    cached_ref,
    pages,
    cache,
    query,
    new,
    decode_query,
    decode_new,
    sections,
    own_rows,
    decode_own_rows,
    scores,
    decode_scores,
    staged,
    decode_staged,
    outbox,
    inbox,
    gathered,
    local_sem,
    send_sem,
    recv_sem,
    part_send_sem,
    part_recv_sem,
    out_send_sem,
    out_recv_sem,
):
    me = lax.axis_index("row")
    page_count, page_rows = pages.shape[0], pages.shape[1]
    per_pair = page_count // count
    prompts, heads = query.shape[:2]
    rows = prompts * heads
    share = gathered.shape[1]
    split = share != rows
    barrier = pltpu.get_barrier_semaphore()
    for step in range(1, count):
        pl.semaphore_signal(
            barrier, inc=1, device_id={"row": partner(me, count, step)}, device_id_type=MESH
        )
    incoming = [
        pltpu.make_async_copy(there, here, local_sem.at[i])
        for i, (there, here) in enumerate(
            (
                (table_hbm, table),
                (pages_hbm, pages),
                (lengths_hbm, lengths_ref),
                (cached_hbm, cached_ref),
                (query_hbm, query),
                (new_hbm, new),
                (cache_hbm, cache),
                (decode_query_hbm, decode_query),
                (decode_new_hbm, decode_new),
            )
        )
    ]
    for copy in incoming:
        copy.start()

    def gather(place, first, width):
        def body(i, carry):
            slot = place * per_pair + first + i
            sections[slot] = pages[source_ref[0, slot]]
            return carry

        lax.fori_loop(0, width, body, 0, unroll=min(8, width))

    page_sends = []

    def send_pages(phase):
        for step, first, width in phase:
            place = partner(me, count, step)
            at = len(page_sends)
            send = pltpu.make_async_remote_copy(
                src_ref=sections.at[pl.ds(place * per_pair + first, width)],
                dst_ref=pool_ref.at[pl.ds(me * per_pair + first, width)],
                send_sem=send_sem.at[at],
                recv_sem=recv_sem.at[at],
                device_id={"row": place},
                device_id_type=MESH,
            )
            send.start()
            page_sends.append(send)

    def exchange(source, target, out_sem, in_sem):
        sends = []
        for step in reversed(range(1, count)):
            place = partner(me, count, step)
            send = pltpu.make_async_remote_copy(
                src_ref=source(place),
                dst_ref=target,
                send_sem=out_sem.at[step - 1],
                recv_sem=in_sem.at[step - 1],
                device_id={"row": place},
                device_id_type=MESH,
            )
            send.start()
            sends.append(send)
        return sends

    phases = plan_phases(count, per_pair)
    incoming[0].wait()
    page = lax.broadcasted_iota(jnp.int32, (page_count, page_count), 0)
    slot = lax.broadcasted_iota(jnp.int32, (page_count, page_count), 1)
    entry = table[...]
    target = lax.div(entry, page_count) * per_pair + lax.rem(entry, per_pair)
    target = jnp.sum(jnp.where(page == slot, target, 0), axis=1, keepdims=True)
    source[...] = jnp.max(jnp.where(target == slot, page, 0), axis=0, keepdims=True)
    listed = pltpu.make_async_copy(source, source_ref, local_sem.at[10])
    listed.start()
    listed.wait()
    incoming[1].wait()
    for at, item in enumerate(phases[0]):
        step, first, width = item
        gather(partner(me, count, step), first, width)
        if at == 0:
            pl.semaphore_wait(barrier, count - 1)
        send_pages([item])
    for step, first, width in phases[1] + phases[2]:
        gather(partner(me, count, step), first, width)
    gather(me, 0, per_pair)
    kept = pltpu.make_async_copy(
        sections.at[pl.ds(me * per_pair, per_pair)],
        pool_ref.at[pl.ds(me * per_pair, per_pair)],
        local_sem.at[9],
    )
    kept.start()

    row = lax.broadcasted_iota(jnp.int32, (rows, LANES), 0)
    lane = lax.broadcasted_iota(jnp.int32, (rows, LANES), 1)
    head_live = lane % 4 == (row // (heads // 2)) % 2
    far = jnp.int32(1 << 30)
    lo = jnp.zeros((rows, LANES), jnp.int32)
    hi = jnp.zeros((rows, LANES), jnp.int32)
    incoming[2].wait()
    incoming[3].wait()
    begin = -me * page_count
    for prompt in range(prompts):
        end = begin + lengths_ref[prompt]
        mine = row // heads == prompt
        lo = jnp.where(mine, begin * page_rows, lo)
        hi = jnp.where(mine, end * page_rows, hi)
        begin = end
    lo = jnp.where(head_live, lo, far)
    own_lo = jnp.where(head_live, (row // heads) * 4, far)
    own_hi = (row // heads) * 4 + 4
    own_lo = jnp.where(me == 0, own_lo, far)
    incoming[4].wait()
    incoming[5].wait()
    own_rows[...] = jnp.zeros_like(own_rows)
    own_rows[: new.shape[0], :] = new[...]
    chunk = 32
    blocks = [(lambda: own_rows[...], LANES, page_count * page_rows, 0, own_lo, own_hi)]
    for at in range(0, page_count, chunk):
        blocks.append(
            (
                lambda at=at: pages[at : at + chunk].reshape(chunk * page_rows, LANES),
                chunk * page_rows,
                at * page_rows,
                at * page_rows,
                lo,
                hi,
            )
        )
    top, total, accumulated = softmax_pass(
        query[...].reshape(rows, LANES), blocks, scores, scaling
    )
    eye = row == lane
    stats = jnp.concatenate(
        [
            jnp.sum(jnp.where(eye, top, 0.0), axis=0, keepdims=True),
            jnp.sum(jnp.where(eye, total, 0.0), axis=0, keepdims=True),
            jnp.zeros((6, LANES), jnp.float32),
        ],
        axis=0,
    )
    for k in range(rows // share):
        outbox[k, :share, :] = accumulated[k * share : (k + 1) * share, :]
        outbox[k, share:, :] = stats
    inbox[me] = outbox[me if split else 0]
    part_sends = exchange(
        lambda place: outbox.at[place if split else 0, pl.ds(0, share + 2)],
        inbox.at[me, pl.ds(0, share + 2)],
        part_send_sem,
        part_recv_sem,
    )
    send_pages(phases[1])

    seqs = decode_query.shape[0]
    cache_rows = cache.shape[1]
    for copy in incoming[6:]:
        copy.wait()
    decode_own_rows[...] = jnp.zeros_like(decode_own_rows)
    for seq in range(seqs):
        for kind in range(2):
            at = seq * 4 + kind * 2
            decode_own_rows[at : at + 2, :] = decode_new[seq, kind].astype(jnp.float32)
    row = lax.broadcasted_iota(jnp.int32, (heads, LANES), 0)
    lane = lax.broadcasted_iota(jnp.int32, (heads, LANES), 1)
    head_live = lane % 4 == (row // (heads // 2)) % 2
    for seq in range(seqs):
        lo = jnp.where(head_live, 0, far)
        hi = jnp.full((heads, LANES), cached_ref[seq] * 4, jnp.int32)
        own_lo = jnp.where(head_live, seq * 4, far)
        own_hi = jnp.full((heads, LANES), seq * 4 + 4, jnp.int32)
        blocks = [
            (
                lambda: decode_own_rows[...].astype(jnp.bfloat16),
                LANES,
                cache_rows,
                0,
                own_lo,
                own_hi,
            ),
            (lambda seq=seq: cache[seq], cache_rows, 0, 0, lo, hi),
        ]
        top, total, accumulated = softmax_pass(decode_query[seq], blocks, decode_scores, scaling)
        decode_staged[seq * heads : (seq + 1) * heads, :] = accumulated / total
    for head in range(heads):
        decode_out_ref[:, head * LANES : (head + 1) * LANES] = decode_staged[
            pl.ds(head, seqs, stride=heads), :
        ].astype(jnp.bfloat16)

    for send in part_sends:
        send.wait_recv()
    base = me * share if split else 0
    row = lax.broadcasted_iota(jnp.int32, (share, LANES), 0)
    lane = lax.broadcasted_iota(jnp.int32, (share, LANES), 1)
    eye = row + base == lane
    top = jnp.full((1, LANES), FLOOR, jnp.float32)
    for k in range(count):
        top = jnp.maximum(top, inbox[k, share : share + 1, :])
    total = jnp.zeros((1, LANES), jnp.float32)
    for k in range(count):
        total = total + inbox[k, share + 1 : share + 2, :] * jnp.exp(
            inbox[k, share : share + 1, :] - top
        )
    joined = jnp.zeros((share, LANES), jnp.float32)
    for k in range(count):
        weight = jnp.exp(inbox[k, share : share + 1, :] - top) / total
        weight = jnp.sum(jnp.where(eye, weight, 0.0), axis=1, keepdims=True)
        joined = joined + inbox[k, :share, :] * weight
    gathered[me if split else 0] = joined.astype(jnp.bfloat16)
    out_sends = []
    if split:
        out_sends = exchange(
            lambda place: gathered.at[me], gathered.at[me], out_send_sem, out_recv_sem
        )
    send_pages(phases[2])
    for send in out_sends:
        send.wait_recv()
    for k in range(rows // share):
        staged[k * share : (k + 1) * share, :] = gathered[k].astype(jnp.float32)
    for head in range(heads):
        prompt_out_ref[:, head * LANES : (head + 1) * LANES] = staged[
            pl.ds(head, prompts, stride=heads), :
        ].astype(jnp.bfloat16)

    kept.wait()
    for send in page_sends:
        send.wait_recv()
    for send in part_sends + out_sends + page_sends:
        send.wait_send()


def write_out(first, second, third, first_out, second_out, third_out, sem):
    copies = [
        pltpu.make_async_copy(here, there, sem.at[i])
        for i, (here, there) in enumerate(
            ((third, third_out), (second, second_out), (first, first_out))
        )
    ]
    for copy in copies:
        copy.start()
    for copy in copies:
        copy.wait()


def per_device(
    prefill_kv,
    page_table,
    prompt_lengths,
    prompt_query,
    prompt_new,
    decode_query,
    decode_new,
    decode_cache,
    cached_lengths,
):
    count = lax.axis_size("row")
    page_count = prefill_kv.shape[0]
    head_depth = prefill_kv.shape[4]
    page_rows = math.prod(prefill_kv.shape[1:4])
    per_pair = page_count // count
    prompts, heads = prompt_query.shape[:2]
    rows = prompts * heads
    share = rows // count if rows % (16 * count) == 0 else rows
    seqs = decode_query.shape[0]
    cache_rows = math.prod(decode_cache.shape[1:4])
    messages = sum(len(phase) for phase in plan_phases(count, per_pair))
    vmem = pl.BlockSpec(memory_space=pltpu.VMEM)
    hbm = pl.BlockSpec(memory_space=pltpu.HBM)
    anywhere = pl.BlockSpec(memory_space=pl.ANY)
    bf16, f32 = jnp.bfloat16, jnp.float32
    out_shape = (
        jax.ShapeDtypeStruct((seqs, heads * head_depth), bf16),
        jax.ShapeDtypeStruct((prompts, heads * head_depth), bf16),
        jax.ShapeDtypeStruct((page_count, page_rows, head_depth), bf16),
    )
    vmem_shape = (
        pltpu.VMEM((seqs, heads * head_depth), bf16),
        pltpu.VMEM((prompts, heads * head_depth), bf16),
        pltpu.VMEM((page_count, page_rows, head_depth), bf16),
    )
    results = pl.pallas_call(
        functools.partial(kernel, count, 1.0 / math.sqrt(head_depth)),
        out_shape=vmem_shape,
        in_specs=[hbm] * 9,
        out_specs=(vmem, vmem, vmem),
        scratch_shapes=[
            pltpu.VMEM((1, page_count), jnp.int32),
            pltpu.VMEM((1, page_count), jnp.int32),
            pltpu.SMEM((1, page_count), jnp.int32),
            pltpu.SMEM(prompt_lengths.shape, jnp.int32),
            pltpu.SMEM(cached_lengths.shape, jnp.int32),
            pltpu.VMEM((page_count, page_rows, head_depth), bf16),
            pltpu.VMEM((seqs, cache_rows, head_depth), bf16),
            pltpu.VMEM(prompt_query.shape, bf16),
            pltpu.VMEM((prompts * 4, head_depth), bf16),
            pltpu.VMEM(decode_query.shape, bf16),
            pltpu.VMEM(decode_new.shape, bf16),
            pltpu.VMEM((page_count, page_rows, head_depth), bf16),
            pltpu.VMEM((LANES, head_depth), bf16),
            pltpu.VMEM((LANES, head_depth), f32),
            pltpu.VMEM((rows, page_count * page_rows + LANES), f32),
            pltpu.VMEM((heads, cache_rows + LANES), f32),
            pltpu.VMEM((rows, head_depth), f32),
            pltpu.VMEM((seqs * heads, head_depth), f32),
            pltpu.VMEM((rows // share, share + 8, LANES), f32),
            pltpu.VMEM((count, share + 8, LANES), f32),
            pltpu.VMEM((rows // share, share, LANES), bf16),
            pltpu.SemaphoreType.DMA((11,)),
            pltpu.SemaphoreType.DMA((messages,)),
            pltpu.SemaphoreType.DMA((messages,)),
            pltpu.SemaphoreType.DMA((count - 1,)),
            pltpu.SemaphoreType.DMA((count - 1,)),
            pltpu.SemaphoreType.DMA((count - 1,)),
            pltpu.SemaphoreType.DMA((count - 1,)),
        ],
        compiler_params=pltpu.CompilerParams(
            collective_id=0, has_side_effects=True, vmem_limit_bytes=58 * 1024 * 1024
        ),
    )(
        page_table.reshape(1, page_count),
        prompt_lengths,
        cached_lengths,
        prefill_kv.reshape(page_count, page_rows, head_depth),
        decode_cache.reshape(seqs, cache_rows, head_depth),
        prompt_query,
        prompt_new.reshape(-1, head_depth),
        decode_query,
        decode_new,
    )
    decode_out, prompt_out, pool = pl.pallas_call(
        write_out,
        out_shape=out_shape,
        in_specs=[vmem] * 3,
        out_specs=(hbm,) * 3,
        scratch_shapes=[pltpu.SemaphoreType.DMA((3,))],
    )(*(pltpu.with_memory_space_constraint(x, pltpu.VMEM) for x in results))
    return decode_out, prompt_out, pool.reshape(prefill_kv.shape)


def solution(mesh):
    in_specs = (
        P(("grp", "row"), None, None, "head", None),
        P(("grp", "row")),
        P("grp"),
        P("grp", "head", None),
        P("grp", None, "head", None),
        P(("grp", "row"), "head", None),
        P(("grp", "row"), None, "head", None),
        P(("grp", "row"), None, None, "head", None),
        P(("grp", "row")),
    )
    out_specs = (
        P(("grp", "row"), "head"),
        P("grp", "head"),
        P(("grp", "row"), None, None, "head", None),
    )
    return jax.shard_map(
        per_device, mesh=mesh, in_specs=in_specs, out_specs=out_specs, check_vma=False
    )
```

```python
import functools
import math

import jax
import jax.numpy as jnp
from jax import lax
from jax.experimental import pallas as pl
from jax.experimental.pallas import tpu as pltpu
from jax.sharding import PartitionSpec as P

MESH = pl.DeviceIdType.MESH
LOWEST = -1e30
FLOOR = -1e29
LANES = 128
CONTRACT_LAST = (((1,), (1,)), ((), ()))


def partner(me, count, step):
    if count & (count - 1):
        return lax.rem(me + step, count)
    place, bit = 0, 1
    while bit < count:
        here = (me // bit) % 2
        place = place + bit * ((1 - here) if step & bit else here)
        bit *= 2
    return place


def softmax_pass(query, blocks, scores_ref, scaling):
    rows = query.shape[0]
    lane = lax.broadcasted_iota(jnp.int32, (rows, LANES), 1)
    peak = jnp.full((rows, LANES), FLOOR, jnp.float32)
    for load, width, at, first, lo, hi in blocks:
        raw = lax.dot_general(query, load(), CONTRACT_LAST, preferred_element_type=jnp.float32)
        for part in range(width // LANES):
            column = lane + (first + part * LANES)
            live = (column >= lo) & (column < hi)
            here = raw[:, part * LANES : (part + 1) * LANES] * scaling
            here = jnp.where(live, here, LOWEST)
            scores_ref[:, pl.ds(at + part * LANES, LANES)] = here
            peak = jnp.maximum(peak, here)
    top = jnp.max(peak, axis=1, keepdims=True)
    total = jnp.zeros((rows, LANES), jnp.float32)
    accumulated = jnp.zeros((rows, LANES), jnp.float32)
    for load, width, at, first, lo, hi in blocks:
        parts = []
        for part in range(width // LANES):
            weight = jnp.exp(scores_ref[:, pl.ds(at + part * LANES, LANES)] - top)
            total = total + weight
            parts.append(pltpu.roll(weight, 2, 1).astype(jnp.bfloat16))
        accumulated = accumulated + jnp.dot(
            jnp.concatenate(parts, axis=1), load(), preferred_element_type=jnp.float32
        )
    return top, jnp.sum(total, axis=1, keepdims=True), accumulated


def plan_phases(count, per_pair):
    pieces = 2 if per_pair % 2 == 0 else 1
    width = per_pair // pieces
    far_steps = [step for step in range(1, count) if step >= count // 2]
    near_steps = [step for step in range(1, count) if step < count // 2]
    far = [(step, piece * width, width) for piece in range(pieces) for step in far_steps]
    near = [(step, piece * width, width) for piece in range(pieces) for step in near_steps]
    f1, f2 = len(far) * 4 // 8, len(far) * 6 // 8
    n1, n2 = len(near) * 2 // 4, len(near) * 4 // 4
    return (far[:f1] + near[:n1], far[f1:f2] + near[n1:n2], far[f2:] + near[n2:])


def kernel(
    count,
    scaling,
    table_hbm,
    lengths_hbm,
    cached_hbm,
    pages_hbm,
    cache_hbm,
    query_hbm,
    new_hbm,
    decode_query_hbm,
    decode_new_hbm,
    decode_out_ref,
    prompt_out_ref,
    pool_ref,
    table,
    source,
    source_ref,
    lengths_ref,
    cached_ref,
    pages,
    cache,
    query,
    new,
    decode_query,
    decode_new,
    sections,
    own_rows,
    decode_own_rows,
    scores,
    decode_scores,
    staged,
    decode_staged,
    outbox,
    inbox,
    gathered,
    local_sem,
    send_sem,
    recv_sem,
    part_send_sem,
    part_recv_sem,
    out_send_sem,
    out_recv_sem,
):
    me = lax.axis_index("row")
    page_count, page_rows = pages.shape[0], pages.shape[1]
    per_pair = page_count // count
    prompts, heads = query.shape[:2]
    rows = prompts * heads
    share = gathered.shape[1]
    split = share != rows
    barrier = pltpu.get_barrier_semaphore()
    for step in range(1, count):
        pl.semaphore_signal(
            barrier, inc=1, device_id={"row": partner(me, count, step)}, device_id_type=MESH
        )
    quarter = page_count // 4

    def part(ref, i):
        return ref.at[pl.ds(i * quarter, quarter)]

    later_pages = [
        pltpu.make_async_copy(part(pages_hbm, i), part(pages, i), local_sem.at[10 + i])
        for i in range(1, 4)
    ]
    incoming = [
        pltpu.make_async_copy(there, here, local_sem.at[i])
        for i, (there, here) in enumerate(
            (
                (table_hbm, table),
                (part(pages_hbm, 0), part(pages, 0)),
                (lengths_hbm, lengths_ref),
                (cached_hbm, cached_ref),
                (query_hbm, query),
                (new_hbm, new),
                (cache_hbm, cache),
                (decode_query_hbm, decode_query),
                (decode_new_hbm, decode_new),
            )
        )
    ]
    for copy in incoming[:2] + later_pages + incoming[2:]:
        copy.start()

    def gather(place, first, width):
        def body(i, carry):
            slot = place * per_pair + first + i
            sections[slot] = pages[source_ref[0, slot]]
            return carry

        lax.fori_loop(0, width, body, 0, unroll=min(8, width))

    page_sends = []

    def send_pages(phase):
        for step, first, width in phase:
            place = partner(me, count, step)
            at = len(page_sends)
            send = pltpu.make_async_remote_copy(
                src_ref=sections.at[pl.ds(place * per_pair + first, width)],
                dst_ref=pool_ref.at[pl.ds(me * per_pair + first, width)],
                send_sem=send_sem.at[at],
                recv_sem=recv_sem.at[at],
                device_id={"row": place},
                device_id_type=MESH,
            )
            send.start()
            page_sends.append(send)

    def exchange(source, target, out_sem, in_sem):
        sends = []
        for step in reversed(range(1, count)):
            place = partner(me, count, step)
            send = pltpu.make_async_remote_copy(
                src_ref=source(place),
                dst_ref=target,
                send_sem=out_sem.at[step - 1],
                recv_sem=in_sem.at[step - 1],
                device_id={"row": place},
                device_id_type=MESH,
            )
            send.start()
            sends.append(send)
        return sends

    phases = plan_phases(count, per_pair)
    incoming[0].wait()
    page = lax.broadcasted_iota(jnp.int32, (page_count, page_count), 0)
    slot = lax.broadcasted_iota(jnp.int32, (page_count, page_count), 1)
    entry = table[...]
    target = lax.div(entry, page_count) * per_pair + lax.rem(entry, per_pair)
    target = jnp.sum(jnp.where(page == slot, target, 0), axis=1, keepdims=True)
    source[...] = jnp.max(jnp.where(target == slot, page, 0), axis=0, keepdims=True)
    listed = pltpu.make_async_copy(source, source_ref, local_sem.at[10])
    listed.start()
    listed.wait()
    for copy in incoming[1:2] + later_pages:
        copy.wait()
    for at, item in enumerate(phases[0]):
        step, first, width = item
        gather(partner(me, count, step), first, width)
        if at == 0:
            pl.semaphore_wait(barrier, count - 1)
        send_pages([item])
    for step, first, width in phases[1] + phases[2]:
        gather(partner(me, count, step), first, width)
    gather(me, 0, per_pair)
    kept = pltpu.make_async_copy(
        sections.at[pl.ds(me * per_pair, per_pair)],
        pool_ref.at[pl.ds(me * per_pair, per_pair)],
        local_sem.at[9],
    )
    kept.start()

    row = lax.broadcasted_iota(jnp.int32, (rows, LANES), 0)
    lane = lax.broadcasted_iota(jnp.int32, (rows, LANES), 1)
    head_live = lane % 4 == (row // (heads // 2)) % 2
    far = jnp.int32(1 << 30)
    lo = jnp.zeros((rows, LANES), jnp.int32)
    hi = jnp.zeros((rows, LANES), jnp.int32)
    incoming[2].wait()
    incoming[3].wait()
    begin = -me * page_count
    for prompt in range(prompts):
        end = begin + lengths_ref[prompt]
        mine = row // heads == prompt
        lo = jnp.where(mine, begin * page_rows, lo)
        hi = jnp.where(mine, end * page_rows, hi)
        begin = end
    lo = jnp.where(head_live, lo, far)
    own_lo = jnp.where(head_live, (row // heads) * 4, far)
    own_hi = (row // heads) * 4 + 4
    own_lo = jnp.where(me == 0, own_lo, far)
    incoming[4].wait()
    incoming[5].wait()
    own_rows[...] = jnp.zeros_like(own_rows)
    own_rows[: new.shape[0], :] = new[...]
    chunk = 32
    blocks = [(lambda: own_rows[...], LANES, page_count * page_rows, 0, own_lo, own_hi)]
    for at in range(0, page_count, chunk):
        blocks.append(
            (
                lambda at=at: pages[at : at + chunk].reshape(chunk * page_rows, LANES),
                chunk * page_rows,
                at * page_rows,
                at * page_rows,
                lo,
                hi,
            )
        )
    top, total, accumulated = softmax_pass(
        query[...].reshape(rows, LANES), blocks, scores, scaling
    )
    eye = row == lane
    stats = jnp.concatenate(
        [
            jnp.sum(jnp.where(eye, top, 0.0), axis=0, keepdims=True),
            jnp.sum(jnp.where(eye, total, 0.0), axis=0, keepdims=True),
            jnp.zeros((6, LANES), jnp.float32),
        ],
        axis=0,
    )
    for k in range(rows // share):
        outbox[k, :share, :] = accumulated[k * share : (k + 1) * share, :]
        outbox[k, share:, :] = stats
    inbox[me] = outbox[me if split else 0]
    part_sends = exchange(
        lambda place: outbox.at[place if split else 0, pl.ds(0, share + 2)],
        inbox.at[me, pl.ds(0, share + 2)],
        part_send_sem,
        part_recv_sem,
    )
    send_pages(phases[1])

    seqs = decode_query.shape[0]
    cache_rows = cache.shape[1]
    for copy in incoming[6:]:
        copy.wait()
    decode_own_rows[...] = jnp.zeros_like(decode_own_rows)
    for seq in range(seqs):
        for kind in range(2):
            at = seq * 4 + kind * 2
            decode_own_rows[at : at + 2, :] = decode_new[seq, kind].astype(jnp.float32)
    row = lax.broadcasted_iota(jnp.int32, (heads, LANES), 0)
    lane = lax.broadcasted_iota(jnp.int32, (heads, LANES), 1)
    head_live = lane % 4 == (row // (heads // 2)) % 2
    for seq in range(seqs):
        lo = jnp.where(head_live, 0, far)
        hi = jnp.full((heads, LANES), cached_ref[seq] * 4, jnp.int32)
        own_lo = jnp.where(head_live, seq * 4, far)
        own_hi = jnp.full((heads, LANES), seq * 4 + 4, jnp.int32)
        blocks = [
            (
                lambda: decode_own_rows[...].astype(jnp.bfloat16),
                LANES,
                cache_rows,
                0,
                own_lo,
                own_hi,
            ),
            (lambda seq=seq: cache[seq], cache_rows, 0, 0, lo, hi),
        ]
        top, total, accumulated = softmax_pass(decode_query[seq], blocks, decode_scores, scaling)
        decode_staged[seq * heads : (seq + 1) * heads, :] = accumulated / total
    for head in range(heads):
        decode_out_ref[:, head * LANES : (head + 1) * LANES] = decode_staged[
            pl.ds(head, seqs, stride=heads), :
        ].astype(jnp.bfloat16)

    for send in part_sends:
        send.wait_recv()
    base = me * share if split else 0
    row = lax.broadcasted_iota(jnp.int32, (share, LANES), 0)
    lane = lax.broadcasted_iota(jnp.int32, (share, LANES), 1)
    eye = row + base == lane
    top = jnp.full((1, LANES), FLOOR, jnp.float32)
    for k in range(count):
        top = jnp.maximum(top, inbox[k, share : share + 1, :])
    total = jnp.zeros((1, LANES), jnp.float32)
    for k in range(count):
        total = total + inbox[k, share + 1 : share + 2, :] * jnp.exp(
            inbox[k, share : share + 1, :] - top
        )
    joined = jnp.zeros((share, LANES), jnp.float32)
    for k in range(count):
        weight = jnp.exp(inbox[k, share : share + 1, :] - top) / total
        weight = jnp.sum(jnp.where(eye, weight, 0.0), axis=1, keepdims=True)
        joined = joined + inbox[k, :share, :] * weight
    gathered[me if split else 0] = joined.astype(jnp.bfloat16)
    out_sends = []
    if split:
        out_sends = exchange(
            lambda place: gathered.at[me], gathered.at[me], out_send_sem, out_recv_sem
        )
    send_pages(phases[2])
    for send in out_sends:
        send.wait_recv()
    for k in range(rows // share):
        staged[k * share : (k + 1) * share, :] = gathered[k].astype(jnp.float32)
    for head in range(heads):
        prompt_out_ref[:, head * LANES : (head + 1) * LANES] = staged[
            pl.ds(head, prompts, stride=heads), :
        ].astype(jnp.bfloat16)

    kept.wait()
    for send in page_sends:
        send.wait_recv()
    for send in part_sends + out_sends + page_sends:
        send.wait_send()


def write_out(first, second, third, first_out, second_out, third_out, sem):
    copies = [
        pltpu.make_async_copy(here, there, sem.at[i])
        for i, (here, there) in enumerate(
            ((third, third_out), (second, second_out), (first, first_out))
        )
    ]
    for copy in copies:
        copy.start()
    for copy in copies:
        copy.wait()


def per_device(
    prefill_kv,
    page_table,
    prompt_lengths,
    prompt_query,
    prompt_new,
    decode_query,
    decode_new,
    decode_cache,
    cached_lengths,
):
    count = lax.axis_size("row")
    page_count = prefill_kv.shape[0]
    head_depth = prefill_kv.shape[4]
    page_rows = math.prod(prefill_kv.shape[1:4])
    per_pair = page_count // count
    prompts, heads = prompt_query.shape[:2]
    rows = prompts * heads
    share = rows // count if rows % (16 * count) == 0 else rows
    seqs = decode_query.shape[0]
    cache_rows = math.prod(decode_cache.shape[1:4])
    messages = sum(len(phase) for phase in plan_phases(count, per_pair))
    vmem = pl.BlockSpec(memory_space=pltpu.VMEM)
    hbm = pl.BlockSpec(memory_space=pltpu.HBM)
    anywhere = pl.BlockSpec(memory_space=pl.ANY)
    bf16, f32 = jnp.bfloat16, jnp.float32
    out_shape = (
        jax.ShapeDtypeStruct((seqs, heads * head_depth), bf16),
        jax.ShapeDtypeStruct((prompts, heads * head_depth), bf16),
        jax.ShapeDtypeStruct((page_count, page_rows, head_depth), bf16),
    )
    vmem_shape = (
        pltpu.VMEM((seqs, heads * head_depth), bf16),
        pltpu.VMEM((prompts, heads * head_depth), bf16),
        pltpu.VMEM((page_count, page_rows, head_depth), bf16),
    )
    results = pl.pallas_call(
        functools.partial(kernel, count, 1.0 / math.sqrt(head_depth)),
        out_shape=vmem_shape,
        in_specs=[hbm] * 9,
        out_specs=(vmem, vmem, vmem),
        scratch_shapes=[
            pltpu.VMEM((1, page_count), jnp.int32),
            pltpu.VMEM((1, page_count), jnp.int32),
            pltpu.SMEM((1, page_count), jnp.int32),
            pltpu.SMEM(prompt_lengths.shape, jnp.int32),
            pltpu.SMEM(cached_lengths.shape, jnp.int32),
            pltpu.VMEM((page_count, page_rows, head_depth), bf16),
            pltpu.VMEM((seqs, cache_rows, head_depth), bf16),
            pltpu.VMEM(prompt_query.shape, bf16),
            pltpu.VMEM((prompts * 4, head_depth), bf16),
            pltpu.VMEM(decode_query.shape, bf16),
            pltpu.VMEM(decode_new.shape, bf16),
            pltpu.VMEM((page_count, page_rows, head_depth), bf16),
            pltpu.VMEM((LANES, head_depth), bf16),
            pltpu.VMEM((LANES, head_depth), f32),
            pltpu.VMEM((rows, page_count * page_rows + LANES), f32),
            pltpu.VMEM((heads, cache_rows + LANES), f32),
            pltpu.VMEM((rows, head_depth), f32),
            pltpu.VMEM((seqs * heads, head_depth), f32),
            pltpu.VMEM((rows // share, share + 8, LANES), f32),
            pltpu.VMEM((count, share + 8, LANES), f32),
            pltpu.VMEM((rows // share, share, LANES), bf16),
            pltpu.SemaphoreType.DMA((14,)),
            pltpu.SemaphoreType.DMA((messages,)),
            pltpu.SemaphoreType.DMA((messages,)),
            pltpu.SemaphoreType.DMA((count - 1,)),
            pltpu.SemaphoreType.DMA((count - 1,)),
            pltpu.SemaphoreType.DMA((count - 1,)),
            pltpu.SemaphoreType.DMA((count - 1,)),
        ],
        compiler_params=pltpu.CompilerParams(
            collective_id=0, has_side_effects=True, vmem_limit_bytes=58 * 1024 * 1024
        ),
    )(
        page_table.reshape(1, page_count),
        prompt_lengths,
        cached_lengths,
        prefill_kv.reshape(page_count, page_rows, head_depth),
        decode_cache.reshape(seqs, cache_rows, head_depth),
        prompt_query,
        prompt_new.reshape(-1, head_depth),
        decode_query,
        decode_new,
    )
    decode_out, prompt_out, pool = pl.pallas_call(
        write_out,
        out_shape=out_shape,
        in_specs=[vmem] * 3,
        out_specs=(hbm,) * 3,
        scratch_shapes=[pltpu.SemaphoreType.DMA((3,))],
    )(*(pltpu.with_memory_space_constraint(x, pltpu.VMEM) for x in results))
    return decode_out, prompt_out, pool.reshape(prefill_kv.shape)


def solution(mesh):
    in_specs = (
        P(("grp", "row"), None, None, "head", None),
        P(("grp", "row")),
        P("grp"),
        P("grp", "head", None),
        P("grp", None, "head", None),
        P(("grp", "row"), "head", None),
        P(("grp", "row"), None, "head", None),
        P(("grp", "row"), None, None, "head", None),
        P(("grp", "row")),
    )
    out_specs = (
        P(("grp", "row"), "head"),
        P("grp", "head"),
        P(("grp", "row"), None, None, "head", None),
    )
    return jax.shard_map(
        per_device, mesh=mesh, in_specs=in_specs, out_specs=out_specs, check_vma=False
    )
```
